512 devices in a mesh: dp: 16 (over y, core), mp: 32 (over x, z).
Axes of the slice: x: 4, y: 8, z: 8, core: 2. Of those that a mesh axis runs over, the one named last changes fastest.
Arguments:
- packed_rows: bfloat16 [16384, 6144], P(('dp', 'mp')), may hold values from -6 to 6
- dest_group: int32 [16384], P(('dp', 'mp')), may hold values from 0 to 15, as said below
- dest_slot: int32 [16384], P(('dp', 'mp')), may hold values from 0 to 31, as said below
- image_ids: int32 [16, 1024], P('dp', 'mp'), may hold values from 0 to 15, never falling along the last dimension, each value on 1 to 512 neighbouring positions
- ln_gain: float32 [6144], replicated, may hold values from 0.1 to 1.9
- qkv_weight: bfloat16 [3, 6144, 4096], P(None, None, 'mp'), may hold values from -0.078125 to 0.078125
- qk_gain: float32 [2, 4096], P(None, 'mp'), may hold values from 0.6 to 8
Outputs:
- attended: bfloat16 [16384, 4096], P(('dp', 'mp'))
The draws below stay inside these ranges and needn't reach their ends.
Inputs may be any that keep to these rules, and one draw needn't show every extreme that they name: `dest_group`: rows of the loader at mp index m go to tokens m * 32 to (m + 1) * 32 - 1 of their group. Each loader device sends at most 4 rows to one group, and in every draw some loader device sends exactly 4 rows to one group. `dest_slot`: together with dest_group, every slot of every receiving device gets exactly one row.
All inputs are finite; a program needn't handle non-finite values.
Results may differ from the reference program's by a relative error of at most 0.022.
The reference program's roundings to bfloat16 on the way (of `grouped`, `normed` and `probs`) count: a program that leaves them out, or rounds other values in their place, can miss the bound.
Values may be sent and summed in bfloat16 or wider, within the bound.
No kernel may reach another device: no remote copies, remote signals or barrier semaphores. Data moves between devices by JAX's collectives and lax.ppermute only.
A program may use at most 64 MiB of HBM per device.

```python
import math
import jax
import jax.numpy as jnp
import numpy as np
from jax import lax

D = 6144
HD = 128
TOK_DEV = 32
H = 32
CAP = 4
GROUP_TOK = 1024
ROWS = 16384
IMAGES = 16
MOST_PATCH = 512
N_DP = 16
N_MP = 32


def packing_plan(key):
    keys = jax.random.split(key, N_MP)

    def column(sub):
        k_shift, k_first, k_tickets, k_order, k_slots = jax.random.split(sub, 5)
        shift = jax.random.permutation(k_shift, N_DP).astype(jnp.int32)
        first = jax.random.randint(k_first, (), 0, N_DP).astype(jnp.int32)
        others = (first + 1 + jnp.arange(N_DP - 1, dtype=jnp.int32)) % N_DP
        tickets = jax.random.permutation(k_tickets, jnp.repeat(others, CAP))[:TOK_DEV - CAP]
        offsets = jnp.concatenate([jnp.full((CAP,), first, jnp.int32), tickets])
        offsets = jax.random.permutation(k_order, offsets)
        slots = jax.random.permutation(k_slots, TOK_DEV).astype(jnp.int32)
        groups = (shift[:, None] + offsets[None, :]) % N_DP
        return (groups, jnp.broadcast_to(slots[None, :], (N_DP, TOK_DEV)))
    groups, slots = jax.vmap(column)(keys)
    groups = jnp.transpose(groups, (1, 0, 2)).reshape(-1).astype(jnp.int32)
    slots = jnp.transpose(slots, (1, 0, 2)).reshape(-1).astype(jnp.int32)
    return (groups, slots)


def draw_dest_group(key, part):
    return packing_plan(key)[0]


def draw_dest_slot(key, part):
    return packing_plan(key)[1]


def draw_qk_gain(key, part):
    key = jax.random.fold_in(key, 7)
    return jax.random.uniform(key, (2, H * HD), jnp.float32, 0.6, 1.4)


def level_of(key, extent, pieces, smallest, high):
    level = 1.0
    for axis_at, blocks in pieces:
        steps = jax.random.uniform(jax.random.fold_in(jax.random.fold_in(key, 6), axis_at), (blocks,), jnp.float32, smallest / len(pieces), high / len(pieces))
        level = level * jnp.repeat(jnp.exp(steps), extent[axis_at] // blocks).reshape((-1,) + (1,) * (len(extent) - 1 - axis_at))
    return level


def split_up(number_of, total, most, lean):
    loads = [(1 << 20) // math.isqrt(grade ** lean) + 1 for grade in range(2, number_of + 1)]
    surplus, holding = total - most - (number_of - 1), [1] * (number_of - 1)
    while surplus > 0:
        candidates = [i for i in range(number_of - 1) if holding[i] < most]
        whole, budget = sum([loads[i] for i in candidates]), surplus
        for i in candidates:
            extra = min(most - holding[i], max(1, budget * loads[i] // whole), surplus)
            holding[i] = holding[i] + extra
            surplus = surplus - extra
    return np.array([most] + holding)


def ragged_sizes(key, number_of, total, most, slope):
    if number_of == 2:
        one = jax.random.randint(key, (), max(1, total - most), min(most, total - 1) + 1)
        return jnp.stack([one, total - one])
    lengths = jnp.asarray(split_up(number_of, total, most, slope), jnp.int32)
    couples = (number_of - 1) // 2
    donor, sink = lengths[1:1 + 2 * couples:2], lengths[2:2 + 2 * couples:2]
    margin = jnp.minimum(donor - 1, most - sink)
    moved = jax.random.randint(jax.random.fold_in(key, 1), (couples,), 0, 1 << 20) % (margin + 1)
    lengths = lengths.at[1:1 + 2 * couples:2].set(donor - moved).at[2:2 + 2 * couples:2].set(sink + moved)
    return lengths[jax.random.permutation(jax.random.fold_in(key, 2), number_of)]


def bell_draw(own_key, extent, scale, bound, cuts=(), kind=jnp.bfloat16):
    entries = jax.random.normal(own_key, extent, jnp.float32) * scale
    if len(cuts) > 0:
        entries = level_of(own_key, extent, cuts, -0.22, 0.18) * entries
    return jnp.clip(entries, min=-bound, max=bound).astype(kind)


def setup_inputs(seed: int = 0) -> dict:
    seeds = jax.random.split(jax.random.key(seed), 8)
    packed_rows = bell_draw(seeds[0], (ROWS, D), 1.0, 6.0, ((0, 512),))
    dest_group = draw_dest_group(jax.random.fold_in(seeds[7], 71), 0)
    dest_slot = draw_dest_slot(jax.random.fold_in(seeds[7], 71), 0)
    image_ids = jax.vmap(lambda own: jnp.searchsorted(jnp.cumsum(ragged_sizes(own, IMAGES, GROUP_TOK, MOST_PATCH, 2)), jnp.arange(GROUP_TOK), side="right"))(jax.random.split(seeds[3], N_DP)).reshape((N_DP, GROUP_TOK)).astype(jnp.int32)
    ln_gain = jnp.clip(1.0 + 0.18 * jax.random.normal(seeds[4], (D,), jnp.float32), 0.1, 1.9)
    qkv_weight = bell_draw(seeds[5], (3, D, H * HD), D ** -0.5, 0.078125, ((2, 32),))
    qk_gain = draw_qk_gain(jax.random.fold_in(seeds[7], 71), 0)
    return dict(packed_rows=packed_rows, dest_group=dest_group, dest_slot=dest_slot, image_ids=image_ids, ln_gain=ln_gain, qkv_weight=qkv_weight, qk_gain=qk_gain)


def norm_rows(rows, gain):
    values = rows.astype(jnp.float32)
    mean = lax.optimization_barrier(jnp.mean(values, axis=-1, keepdims=True))
    centered = values - mean
    spread = lax.optimization_barrier(jnp.mean(centered * centered, axis=-1, keepdims=True))
    return (centered * lax.rsqrt(spread + 1e-06) * gain.astype(jnp.float32)).astype(jnp.bfloat16)

def one_group(normed_rows, group_ids, qkv_weight, qk_gain):
    count = normed_rows.shape[0]
    heads = qkv_weight.shape[2] // HD
    query = jnp.dot(normed_rows, qkv_weight[0], preferred_element_type=jnp.float32).reshape(count, heads, HD)
    key = jnp.dot(normed_rows, qkv_weight[1], preferred_element_type=jnp.float32).reshape(count, heads, HD)
    value = jnp.dot(normed_rows, qkv_weight[2], preferred_element_type=jnp.float32).astype(jnp.bfloat16).reshape(count, heads, HD)
    query_n = norm_rows(query, qk_gain[0].reshape(heads, HD))
    key_n = norm_rows(key, qk_gain[1].reshape(heads, HD))
    scores = jnp.einsum('qhc,khc->hqk', query_n.astype(jnp.float32), key_n.astype(jnp.float32)) * HD ** (-0.5)
    same = group_ids[:, None] == group_ids[None, :]
    masked = jnp.where(same[None], scores, -1e+30)
    top = lax.optimization_barrier(jnp.max(masked, axis=-1, keepdims=True))
    weights = jnp.exp(masked - top)
    probs = (weights / lax.optimization_barrier(jnp.sum(weights, axis=-1, keepdims=True))).astype(jnp.bfloat16)
    result = jnp.einsum('hqk,khc->qhc', probs.astype(jnp.float32), value.astype(jnp.float32))
    return result.astype(jnp.bfloat16).reshape(count, heads * HD)

def reference(packed_rows, dest_group, dest_slot, image_ids, ln_gain, qkv_weight, qk_gain):
    index = jnp.arange(packed_rows.shape[0], dtype=jnp.int32)
    column = index // TOK_DEV % N_MP
    target = (dest_group * GROUP_TOK + column * TOK_DEV + dest_slot).astype(jnp.int32)
    grouped = jnp.zeros_like(packed_rows).at[target].set(packed_rows)
    normed = norm_rows(grouped, ln_gain).reshape(N_DP, GROUP_TOK, packed_rows.shape[1])

    def apply_group(pair):
        return one_group(pair[0], pair[1], qkv_weight, qk_gain)
    attended = lax.map(apply_group, (normed, image_ids))
    return attended.reshape(N_DP * GROUP_TOK, qkv_weight.shape[2])
```

```python
import functools

import jax
import jax.numpy as jnp
import numpy as np
from jax import lax
from jax.experimental import pallas as pl
from jax.experimental.pallas import tpu as pltpu
from jax.sharding import PartitionSpec as P

HD = 128
LANES = 128
NX, NZ = 4, 8
AXES = ("dp", "mp")
BF16 = jnp.bfloat16
F32 = jnp.float32
VMEM = pltpu.VMEM
SMEM = pltpu.SMEM


def vmem_call(body, outs, n_in, scratch=(), smem_in=(), limit=48):
    return pl.pallas_call(
        body,
        out_shape=outs,
        in_specs=[
            pl.BlockSpec(memory_space=SMEM if i in smem_in else VMEM) for i in range(n_in)
        ],
        out_specs=jax.tree.map(lambda _: pl.BlockSpec(memory_space=VMEM), outs),
        scratch_shapes=scratch,
        compiler_params=pltpu.CompilerParams(vmem_limit_bytes=limit << 20),
    )


def pairs(n_dp, move):
    out = []
    for dp in range(n_dp):
        for mp in range(NX * NZ):
            c, x, z = move(dp % 2, mp // NZ, mp % NZ)
            out.append((dp * NX * NZ + mp, (dp // 2 * 2 + c) * NX * NZ + x * NZ + z))
    return out


def send(array, n_dp, move):
    return lax.ppermute(array, AXES, pairs(n_dp, move))


def along_z(c, x, z):
    return c, x, (z + (1 if c == 0 else -1)) % NZ


def across_x(c, x, z):
    return c, x ^ 1, z


def mirror_x(c, x, z):
    return c, 3 - x, z


def other_core(c, x, z):
    return 1 - c, x, z


def to_region(c, x, z):
    return (c, x, z) if c == x // 2 else (1 - c, 3 - x, z)


def block_columns():
    table = np.zeros((2, NX, NZ, NX * NZ), np.int32)
    for c in range(2):
        for x in range(NX):
            for z in range(NZ):
                cols = []
                for mine in (c, 1 - c):
                    turn = 1 if mine == 0 else -1
                    held = [(x, z, mine), (x ^ 1, z, mine)]
                    for s in (1, 2, 3):
                        for xx in (x, x ^ 1):
                            for core in (mine, 1 - mine):
                                held.append((xx, (z - turn * s) % NZ, core))
                    held += [(x, (z + 4) % NZ, mine), (x ^ 1, (z + 4) % NZ, mine)]
                    for xx, zz, core in held:
                        cols.append((xx if core == xx // 2 else 3 - xx) * NZ + zz)
                table[c, x, z] = cols
    return table.reshape(2, NX * NZ, NX * NZ)


def norm_rows(values, gain):
    mean = jnp.mean(values, axis=-1, keepdims=True)
    centered = values - mean
    spread = jnp.mean(centered * centered, axis=-1, keepdims=True)
    return (centered * lax.rsqrt(spread + 1e-06) * gain).astype(BF16)


def pack_body(capacity, rows, group_col, group_row, slot_row, gain, out):
    tok, width = rows.shape
    slots = out.shape[0]
    normed = norm_rows(rows[...].astype(F32), gain[...])
    i = lax.broadcasted_iota(jnp.int32, (tok, tok), 0)
    j = lax.broadcasted_iota(jnp.int32, (tok, tok), 1)
    earlier = (group_col[...] == group_row[...]) & (i < j)
    rank = jnp.sum(jnp.where(earlier, 1, 0), axis=0, keepdims=True)
    target = group_row[...] * capacity + rank
    hit = lax.broadcasted_iota(jnp.int32, (slots, tok), 0) == target
    onehot = jnp.where(hit, 1.0, 0.0)
    out[:, :width] = jnp.dot(
        onehot.astype(BF16), normed, preferred_element_type=F32
    ).astype(BF16)
    slot = jnp.sum(onehot * (slot_row[...].astype(F32) + 1.0), axis=1, keepdims=True) - 1.0
    out[:, width:] = jnp.broadcast_to(slot, (slots, LANES)).astype(BF16)


def place_body(got, ids_col, out):
    tok = out.shape[0]
    width = out.shape[1] - LANES
    slot = got[:, width:].astype(F32)[:, :tok]
    hit = slot == lax.broadcasted_iota(jnp.int32, slot.shape, 1).astype(F32)
    onehot = jnp.where(hit, 1.0, 0.0).astype(BF16)
    out[:, :width] = lax.dot_general(
        onehot, got[:, :width], (((0,), (0,)), ((), ())), preferred_element_type=F32
    ).astype(BF16)
    out[:, width:] = jnp.broadcast_to(ids_col[...].astype(F32), (tok, LANES)).astype(BF16)


def proj_body(n_a, place, *refs):
    a_refs, refs = refs[:n_a], refs[n_a:]
    b_refs, refs = refs[:n_a], refs[n_a:]
    (where_am_i, w_own, w_near, w_far, gain_own, gain_imp, mine, other, tokens, total) = refs
    da = a_refs[0].shape[1]
    width = tokens.shape[1]
    half = width // 2
    for a_ref, b_ref, (a_pieces, b_pieces) in zip(a_refs, b_refs, place):
        for src, dst, n in a_pieces:
            tokens[dst : dst + n, :da] = a_ref[src : src + n, :]
        for src, dst, n in b_pieces:
            tokens[dst : dst + n, da:] = b_ref[src : src + n, : width - da]
            ids = b_ref[src : src + n, width - da :]
            mine[dst : dst + n, 3 * HD :] = ids
            other[dst : dst + n, 3 * HD :] = ids
    core = where_am_i[0]
    step = min(512, half)
    for h, w_imp in enumerate((w_near, w_far)):
        base = (core if h == 0 else 1 - core) * half
        for k in range(half // step):
            at = pl.multiple_of(base + k * step, step)
            lhs = tokens[:, pl.ds(at, step)]
            own = [w_own[j, pl.ds(at, step), :] for j in range(3)]
            imp = [w_imp[j, k * step : (k + 1) * step, :] for j in range(3)]
            six = own + imp
            for n in range(3):
                w = jnp.concatenate(six[2 * n : 2 * n + 2], axis=1)
                part = jnp.dot(lhs, w, preferred_element_type=F32)
                cols = slice(2 * n * HD, (2 * n + 2) * HD)
                if h == 0 and k == 0:
                    total[:, cols] = part
                else:
                    total[:, cols] += part
    home = where_am_i[1] == 1

    def emit(first, second):
        for start, gain, dst in ((0, gain_own, first), (3 * HD, gain_imp, second)):
            for j in range(2):
                cols = total[:, start + j * HD : start + (j + 1) * HD]
                dst[:, j * HD : (j + 1) * HD] = norm_rows(cols, gain[j : j + 1, :])
            dst[:, 2 * HD : 3 * HD] = total[:, start + 2 * HD : start + 3 * HD].astype(BF16)

    @pl.when(home)
    def _():
        emit(mine, other)

    @pl.when(jnp.logical_not(home))
    def _():
        emit(other, mine)


def attend_body(tok, column, first, second, out, ids_row):
    rows = first.shape[0]
    for n, half in enumerate((first, second)):
        turned = jnp.transpose(half[:, 3 * HD :].astype(F32))
        ids_row[:, n * rows : (n + 1) * rows] = turned[0:8, :]
    key = jnp.concatenate([first[:, HD : 2 * HD], second[:, HD : 2 * HD]], axis=0)
    value = jnp.concatenate([first[:, 2 * HD : 3 * HD], second[:, 2 * HD : 3 * HD]], axis=0)
    step = min(256, rows)
    for n, half in enumerate((first, second)):
        for at in range(0, rows, step):
            query = half[at : at + step, :HD]
            scores = lax.dot_general(
                query, key, (((1,), (1,)), ((), ())), preferred_element_type=F32
            ) * HD ** (-0.5)
            same = half[at : at + step, 3 * HD : 3 * HD + 1].astype(F32) == ids_row[0:1, :]
            masked = jnp.where(same, scores, -1e30)
            top = jnp.max(masked, axis=-1, keepdims=True)
            weights = jnp.exp(masked - top)
            probs = (weights / jnp.sum(weights, axis=-1, keepdims=True)).astype(BF16)
            result = jnp.dot(probs, value, preferred_element_type=F32).astype(BF16)
            for b in range(step // tok):
                block = (n * rows + at) // tok + b
                out[column[block]] = result[b * tok : (b + 1) * tok, :]


def local(packed_rows, dest_group, dest_slot, image_ids, ln_gain, qkv_weight, qk_gain):
    tok, width = packed_rows.shape
    n_dp = lax.axis_size("dp")
    capacity = max(2, 2 * tok // n_dp)
    dp, mp = lax.axis_index("dp"), lax.axis_index("mp")
    c = dp % 2
    home = c == mp // NZ // 2
    half = width // 2
    go = functools.partial(lambda array, move: send(array, n_dp, move))

    near = go(lax.dynamic_slice_in_dim(qkv_weight, c * half, half, axis=1), mirror_x)
    far = go(near, other_core)
    gain_imp = go(qk_gain, mirror_x)

    packed = vmem_call(
        functools.partial(pack_body, capacity),
        jax.ShapeDtypeStruct((n_dp * capacity, width + LANES), BF16),
        5,
    )(packed_rows, dest_group[:, None], dest_group[None, :], dest_slot[None, :], ln_gain[None, :])
    got = lax.all_to_all(
        packed.reshape(n_dp, capacity, width + LANES), "dp", split_axis=0, concat_axis=0, tiled=True
    ).reshape(n_dp * capacity, width + LANES)
    placed = vmem_call(
        place_body, jax.ShapeDtypeStruct((tok, width + LANES), BF16), 2
    )(got, image_ids.reshape(tok, 1))

    da = width * 13 // 24 // 256 * 256
    moved = go(placed, to_region)
    twin = go(moved, other_core)
    a, b = moved[:, :da], moved[:, da:]
    b_x = go(b, across_x)
    b_x_twin = go(b_x, other_core)
    a_now = jnp.concatenate([a, twin[:, :da]], axis=0)
    b_now = jnp.concatenate([b, twin[:, da:], b_x, b_x_twin], axis=0)
    a_held, b_held = [a], [b_now]
    for s in range(1, 5):
        if s == 4:
            a_now = a_now[:tok]
            b_now = jnp.concatenate([b_now[:tok], b_now[2 * tok : 3 * tok]], axis=0)
        a_now = go(a_now, along_z)
        b_now = go(b_now, along_z)
        a_held.append(a_now)
        b_held.append(b_now)
    x01 = go(jnp.concatenate(a_held[:2], axis=0), across_x)
    a_x = [x01] + [go(held, across_x) for held in a_held[2:]]

    t = tok
    a_list = a_held + a_x
    a_place = [
        [(0, 0, t)], [(0, 2 * t, 2 * t)], [(0, 6 * t, 2 * t)], [(0, 10 * t, 2 * t)], [(0, 14 * t, t)],
        [(0, t, t), (t, 4 * t, 2 * t)], [(0, 8 * t, 2 * t)], [(0, 12 * t, 2 * t)], [(0, 15 * t, t)],
    ]
    b_place = [
        [(0, 0, t), (2 * t, t, t)], [(0, 2 * t, 4 * t)], [(0, 6 * t, 4 * t)], [(0, 10 * t, 4 * t)],
        [(0, 14 * t, 2 * t)],
    ]
    b_list = b_held + [b_held[-1]] * (len(a_list) - len(b_held))
    b_place = b_place + [[]] * (len(a_list) - len(b_place))
    here = jnp.stack([c, home.astype(jnp.int32)]).astype(jnp.int32)
    rows = 16 * tok
    shape = jax.ShapeDtypeStruct((rows, 4 * HD), BF16)
    n_a = len(a_list)
    mine, other = vmem_call(
        functools.partial(proj_body, n_a, list(zip(a_place, b_place))),
        (shape, shape),
        2 * n_a + 6,
        scratch=[VMEM((rows, width), BF16), VMEM((rows, 6 * HD), F32)],
        smem_in=(2 * n_a,),
        limit=56,
    )(*a_list, *b_list, here, qkv_weight, near, far, qk_gain, gain_imp)
    swapped = go(other, other_core)

    table = jnp.asarray(block_columns())
    column = lax.dynamic_slice(table, (c, mp, 0), (1, 1, NX * NZ)).reshape(NX * NZ)
    result = vmem_call(
        functools.partial(attend_body, tok),
        jax.ShapeDtypeStruct((NX * NZ, tok, HD), BF16),
        3,
        scratch=[VMEM((8, 2 * rows), F32)],
        smem_in=(0,),
    )(column, mine, swapped)

    back = lax.all_to_all(result, "mp", split_axis=0, concat_axis=0, tiled=True)
    low, high = back[: NX * NZ // 2], back[NX * NZ // 2 :]
    first = c == 0
    keep = jnp.where(first, low, high)
    gave = go(jnp.where(first, high, low), other_core)
    gave = jnp.concatenate([gave[NZ:], gave[:NZ]], axis=0)
    heads = jnp.concatenate([jnp.where(first, keep, gave), jnp.where(first, gave, keep)], axis=0)
    return jnp.transpose(heads, (1, 0, 2)).reshape(tok, NX * NZ * HD)


def solution(mesh):
    return jax.shard_map(
        local,
        mesh=mesh,
        in_specs=(
            P(("dp", "mp"), None),
            P(("dp", "mp")),
            P(("dp", "mp")),
            P("dp", "mp"),
            P(),
            P(None, None, "mp"),
            P(None, "mp"),
        ),
        out_specs=P(("dp", "mp"), None),
        check_vma=False,
    )
```

```python
import functools

import jax
import jax.numpy as jnp
from jax import lax
from jax.experimental import pallas as pl
from jax.experimental.pallas import tpu as pltpu
from jax.sharding import Mesh
from jax.sharding import PartitionSpec as P

HD = 128
LANES = 128
NX, NZ = 4, 8
AXES = ("y", "core", "half", "side", "z")
BF16 = jnp.bfloat16
F32 = jnp.float32
VMEM = pltpu.VMEM
SMEM = pltpu.SMEM


def vmem_call(body, outs, n_in, scratch=(), smem_in=(), hbm_in=(), limit=48):
    spaces = [SMEM if i in smem_in else pl.ANY if i in hbm_in else VMEM for i in range(n_in)]
    return pl.pallas_call(
        body,
        out_shape=outs,
        in_specs=[pl.BlockSpec(memory_space=space) for space in spaces],
        out_specs=jax.tree.map(lambda _: pl.BlockSpec(memory_space=VMEM), outs),
        scratch_shapes=scratch,
        compiler_params=pltpu.CompilerParams(vmem_limit_bytes=limit << 20),
    )


def pairs(n_dp, move):
    out = []
    for dp in range(n_dp):
        for mp in range(NX * NZ):
            to = move(dp % 2, mp // NZ, mp % NZ)
            if to is None:
                continue
            c, x, z = to
            out.append((dp * NX * NZ + mp, (dp // 2 * 2 + c) * NX * NZ + x * NZ + z))
    return out


def send(array, n_dp, move):
    return lax.ppermute(array, AXES, pairs(n_dp, move))


def other_core(c, x, z):
    return 1 - c, x, z


def to_region(c, x, z):
    return None if c == x // 2 else (1 - c, 3 - x, z)


def after(array, *earlier):
    return lax.optimization_barrier((array, *earlier))[0]


def norm_rows(values, gain):
    mean = jnp.mean(values, axis=-1, keepdims=True)
    centered = values - mean
    spread = jnp.mean(centered * centered, axis=-1, keepdims=True)
    return (centered * lax.rsqrt(spread + 1e-06) * gain).astype(BF16)


def pack_body(rows, group_row, slot_row, gain, out):
    tok, width = rows.shape
    groups, capacity, _ = out.shape
    slots = groups * capacity
    normed = norm_rows(rows[...].astype(F32), gain[...])
    i = lax.broadcasted_iota(jnp.int32, (tok, tok), 0)
    j = lax.broadcasted_iota(jnp.int32, (tok, tok), 1)
    across = jnp.broadcast_to(group_row[...], (tok, tok)).astype(F32)
    down = jnp.sum(jnp.where(i == j, across, 0.0), axis=1, keepdims=True)
    rank = jnp.sum(jnp.where((down == across) & (i < j), 1, 0), axis=0, keepdims=True)
    target = group_row[...] * capacity + rank
    hit = lax.broadcasted_iota(jnp.int32, (slots, tok), 0) == target
    onehot = jnp.where(hit, 1.0, 0.0)
    sent = jnp.dot(onehot.astype(BF16), normed, preferred_element_type=F32).astype(BF16)
    slot = jnp.sum(onehot * (slot_row[...].astype(F32) + 1.0), axis=1, keepdims=True) - 1.0
    slot = jnp.broadcast_to(slot, (slots, LANES)).astype(BF16)
    for g in range(groups):
        out[g, :, :width] = sent[g * capacity : (g + 1) * capacity, :]
        out[g, :, width:] = slot[g * capacity : (g + 1) * capacity, :]


def place_body(got, ids_col, out):
    tok = out.shape[0]
    width = out.shape[1] - LANES
    slot = got[:, width:].astype(F32)[:, :tok]
    hit = slot == lax.broadcasted_iota(jnp.int32, slot.shape, 1).astype(F32)
    onehot = jnp.where(hit, 1.0, 0.0).astype(BF16)
    out[:, :width] = lax.dot_general(
        onehot, got[:, :width], (((0,), (0,)), ((), ())), preferred_element_type=F32
    ).astype(BF16)
    out[:, width:] = jnp.broadcast_to(ids_col[...].astype(F32), (tok, LANES)).astype(BF16)


def attend_body(place, tokens, ids, weight, gain, out, total, normed, ids_row):
    k = pl.program_id(0)
    rows = tokens.shape[0]
    tok = out.shape[1]
    three = jnp.concatenate([weight[j] for j in range(3)], axis=1)
    part = jnp.dot(tokens[...], three, preferred_element_type=F32)

    @pl.when(k == 0)
    def _():
        total[...] = part
        ids_row[...] = jnp.transpose(ids[...].astype(F32))[0:8, :]

    @pl.when(k > 0)
    def _():
        total[...] += part

    @pl.when(k == pl.num_programs(0) - 1)
    def _():
        for j in range(2):
            cols = slice(j * HD, (j + 1) * HD)
            normed[:, cols] = norm_rows(total[:, cols], gain[j : j + 1, :])
        normed[:, 2 * HD :] = total[:, 2 * HD :].astype(BF16)
        key, value = normed[:, HD : 2 * HD], normed[:, 2 * HD :]
        half = place[0]
        step = min(256, rows)
        for at in range(0, rows, step):
            scores = lax.dot_general(
                normed[at : at + step, :HD], key, (((1,), (1,)), ((), ())), preferred_element_type=F32
            ) * HD ** (-0.5)
            same = ids[at : at + step, 0:1].astype(F32) == ids_row[0:1, :]
            masked = jnp.where(same, scores, -1e30)
            top = jnp.max(masked, axis=-1, keepdims=True)
            weights = jnp.exp(masked - top)
            probs = (weights / jnp.sum(weights, axis=-1, keepdims=True)).astype(BF16)
            result = jnp.dot(probs, value, preferred_element_type=F32).astype(BF16)
            for b in range(step // tok):
                block = at // tok + b
                core, side, z = block // (2 * NZ), block // NZ % 2, block % NZ
                x = jnp.where(half == core, 2 * half + side, 3 - 2 * half - side)
                out[x * NZ + z] = result[b * tok : (b + 1) * tok, :]


def local(packed_rows, dest_group, dest_slot, image_ids, ln_gain, qkv_weight, qk_gain):
    tok, width = packed_rows.shape
    n_dp = 2 * lax.axis_size("y")
    capacity = max(2, 2 * tok // n_dp)
    c = lax.axis_index("core")
    on_half = lax.axis_index("half")
    home = c == on_half
    go = functools.partial(lambda array, move: send(array, n_dp, move))

    packed = pl.pallas_call(
        pack_body,
        grid=(1,),
        out_shape=jax.ShapeDtypeStruct((n_dp, capacity, width + LANES), BF16),
        compiler_params=pltpu.CompilerParams(vmem_limit_bytes=32 << 20),
    )(packed_rows, dest_group[None, :], dest_slot[None, :], ln_gain[None, :])
    got = lax.all_to_all(packed, ("y", "core"), split_axis=0, concat_axis=0, tiled=True)
    placed = vmem_call(
        place_body, jax.ShapeDtypeStruct((tok, width + LANES), BF16), 2
    )(got.reshape(n_dp * capacity, width + LANES), image_ids.reshape(tok, 1))

    moved = jnp.where(home, placed, go(placed, to_region))
    gathered = lax.all_gather(moved, ("core", "side", "z"), axis=0, tiled=True)
    weight = jnp.where(home, qkv_weight, go(after(qkv_weight, moved), to_region))
    gain = jnp.where(home, qk_gain, go(after(qk_gain, moved), to_region))

    rows = gathered.shape[0]
    step = width // 6
    result = pl.pallas_call(
        attend_body,
        grid=(width // step,),
        out_shape=jax.ShapeDtypeStruct((rows // tok, tok, HD), BF16),
        in_specs=[
            pl.BlockSpec(memory_space=SMEM),
            pl.BlockSpec((rows, step), lambda k: (0, k)),
            pl.BlockSpec((rows, LANES), lambda k: (0, width // LANES)),
            pl.BlockSpec((3, step, HD), lambda k: (0, k, 0)),
            pl.BlockSpec(memory_space=VMEM),
        ],
        out_specs=pl.BlockSpec(memory_space=VMEM),
        scratch_shapes=[
            VMEM((rows, 3 * HD), F32), VMEM((rows, 3 * HD), BF16), VMEM((8, rows), F32)
        ],
        compiler_params=pltpu.CompilerParams(vmem_limit_bytes=48 << 20),
    )(on_half[None], gathered, gathered, weight, gain)

    back = lax.all_to_all(result, ("half", "side", "z"), split_axis=0, concat_axis=0, tiled=True)
    low, high = back[: NX * NZ // 2], back[NX * NZ // 2 :]
    first = c == 0
    keep = jnp.where(first, low, high)
    gave = go(jnp.where(first, high, low), other_core)
    gave = jnp.concatenate([gave[NZ:], gave[:NZ]], axis=0)
    heads = jnp.concatenate([jnp.where(first, keep, gave), jnp.where(first, gave, keep)], axis=0)
    return jnp.transpose(heads, (1, 0, 2)).reshape(tok, NX * NZ * HD)


def solution(mesh):
    n_dp = mesh.devices.shape[0]
    split = Mesh(mesh.devices.reshape(n_dp // 2, 2, 2, NX // 2, NZ), AXES)
    dp, mp = ("y", "core"), ("half", "side", "z")
    return jax.shard_map(
        local,
        mesh=split,
        in_specs=(P(AXES, None), P(AXES), P(AXES), P(dp, mp), P(), P(None, None, mp), P(None, mp)),
        out_specs=P(AXES, None),
        check_vma=False,
    )
```

```python
import functools

import jax
import jax.numpy as jnp
from jax import lax
from jax.experimental import pallas as pl
from jax.experimental.pallas import tpu as pltpu
from jax.sharding import Mesh
from jax.sharding import PartitionSpec as P

HD = 128
LOG2_E = 1.4426950408889634
LANES = 128
NX, NZ = 4, 8
AXES = ("y", "core", "half", "side", "z")
BF16 = jnp.bfloat16
F32 = jnp.float32
VMEM = pltpu.VMEM
SMEM = pltpu.SMEM


def vmem_call(body, outs, n_in, scratch=(), smem_in=(), hbm_in=(), limit=48):
    spaces = [SMEM if i in smem_in else pl.ANY if i in hbm_in else VMEM for i in range(n_in)]
    return pl.pallas_call(
        body,
        out_shape=outs,
        in_specs=[pl.BlockSpec(memory_space=space) for space in spaces],
        out_specs=jax.tree.map(lambda _: pl.BlockSpec(memory_space=VMEM), outs),
        scratch_shapes=scratch,
        compiler_params=pltpu.CompilerParams(vmem_limit_bytes=limit << 20),
    )


def pairs(n_dp, move):
    out = []
    for dp in range(n_dp):
        for mp in range(NX * NZ):
            to = move(dp % 2, mp // NZ, mp % NZ)
            if to is None:
                continue
            c, x, z = to
            out.append((dp * NX * NZ + mp, (dp // 2 * 2 + c) * NX * NZ + x * NZ + z))
    return out


def send(array, n_dp, move):
    return lax.ppermute(array, AXES, pairs(n_dp, move))


def to_next(c, x, z):
    return (0, x ^ 1, z) if c == 0 else (1, 3 - x, z)


def opposite_x(c, x, z):
    return c, x ^ 2, z


def on_by_side(c, x, z):
    return (1, x ^ 1, z) if c == 1 else None


def on_by_mirror(c, x, z):
    return (1, 3 - x, z) if c == 0 else None


EXCHANGE = (
    lambda c, x, z: (1, x, z) if c == 0 else (0, 3 - x, z),
    lambda c, x, z: (0, x ^ 1, z) if c == 0 else (1, 3 - x, z),
    lambda c, x, z: (1, x ^ 1, z) if c == 0 else (0, x ^ 2, z),
    lambda c, x, z: None if c == 0 else (1, x ^ 2, z),
)


def after(array, *earlier):
    return lax.optimization_barrier((array, *earlier))[0]


def norm_rows(values, gain):
    mean = jnp.mean(values, axis=-1, keepdims=True)
    centered = values - mean
    spread = jnp.mean(centered * centered, axis=-1, keepdims=True)
    return (centered * lax.rsqrt(spread + 1e-06) * gain).astype(BF16)


def pack_body(rows, plan, weight, out, first_two, sem):
    copy = pltpu.make_async_copy(weight.at[0:2], first_two, sem)
    copy.start()
    tok, width = rows.shape
    groups, capacity, _ = out.shape
    slots = groups * capacity
    group_row, slot_row = plan[0:1, :], plan[1:2, :]
    i = lax.broadcasted_iota(jnp.int32, (tok, tok), 0)
    j = lax.broadcasted_iota(jnp.int32, (tok, tok), 1)
    across = jnp.broadcast_to(group_row, (tok, tok)).astype(F32)
    down = jnp.sum(jnp.where(i == j, across, 0.0), axis=1, keepdims=True)
    rank = jnp.sum(jnp.where((down == across) & (i < j), 1, 0), axis=0, keepdims=True)
    target = group_row * capacity + rank
    hit = lax.broadcasted_iota(jnp.int32, (slots, tok), 0) == target
    onehot = jnp.where(hit, 1.0, 0.0)
    sent = jnp.dot(onehot.astype(BF16), rows[...], preferred_element_type=F32).astype(BF16)
    slot = jnp.sum(onehot * (slot_row.astype(F32) + 1.0), axis=1, keepdims=True) - 1.0
    slot = jnp.broadcast_to(slot, (slots, LANES)).astype(BF16)
    for g in range(groups):
        out[g, :, :width] = sent[g * capacity : (g + 1) * capacity, :]
        out[g, :, width:] = slot[g * capacity : (g + 1) * capacity, :]
    copy.wait()


def place_body(got, ids_col, gain, out):
    tok = out.shape[0]
    width = out.shape[1] - LANES
    slot = got[:, width:].astype(F32)[:, :tok]
    hit = slot == lax.broadcasted_iota(jnp.int32, slot.shape, 1).astype(F32)
    onehot = jnp.where(hit, 1.0, 0.0).astype(BF16)
    grouped = lax.dot_general(
        onehot, got[:, :width], (((0,), (0,)), ((), ())), preferred_element_type=F32
    )
    out[:, :width] = norm_rows(grouped, gain[...])
    out[:, width:] = jnp.broadcast_to(ids_col[...].astype(F32), (tok, LANES)).astype(BF16)


def project_body(place, tokens, ids, own, nqk, nv, fq, fk, fv0, fv1, gain, *refs):
    outs, total = refs[:5], refs[5]
    k = pl.program_id(0)
    steps = pl.num_programs(0)
    rows = tokens.shape[0] // 2
    first_core = place[0] == 0
    near = [nqk[0], nqk[1], nv[...]]
    far = [fq[...], fk[...], jnp.where(k < steps // 2, fv0[...], fv1[...])]
    six = [jnp.where(first_core, own[j], near[j]) for j in range(3)]
    six += [jnp.where(first_core, near[j], far[j]) for j in range(3)]
    part = jnp.dot(tokens[...], jnp.concatenate(six, axis=1), preferred_element_type=F32)

    @pl.when(k == 0)
    def _():
        total[...] = part

    @pl.when(k > 0)
    def _():
        total[...] += part

    def emit(dsts):
        turned = jnp.transpose(ids[...].astype(F32))[0:16, :].astype(BF16)
        for n, dst in enumerate(dsts):
            head, group = n // 2, n % 2
            at = slice(group * rows, (group + 1) * rows)
            for j in range(2):
                cols = total[at, (3 * head + j) * HD : (3 * head + j + 1) * HD]
                dst[:rows, j * HD : (j + 1) * HD] = norm_rows(
                    cols, gain[2 * head + j : 2 * head + j + 1, :]
                )
            dst[:rows, 2 * HD :] = total[at, (3 * head + 2) * HD : (3 * head + 3) * HD].astype(BF16)
            dst[rows:, :rows] = turned[:, at]
            dst[rows:, rows:] = jnp.zeros((16, 3 * HD - rows), BF16)

    @pl.when((k == steps - 1) & first_core)
    def _():
        emit(outs[:4])
        outs[4][...] = jnp.zeros_like(outs[4])

    @pl.when((k == steps - 1) & jnp.logical_not(first_core))
    def _():
        outs[0][...] = jnp.zeros_like(outs[0])
        emit(outs[1:])


def attend_body(place, kept, got0, got1, got2, got3, out, qkv, ids_row, ids_col):
    rows = kept.shape[0] - 16
    tok = out.shape[1]
    per = rows // tok
    first_core = place[0] == 0
    for n, (a, b) in enumerate(((kept, got0), (got0, got1), (got1, got2), (got2, got3))):
        at = slice(n * rows, (n + 1) * rows)
        qkv[at, :] = jnp.where(first_core, a[:rows, :], b[:rows, :])
        packed = jnp.where(first_core, a[rows:, :rows], b[rows:, :rows]).astype(F32)
        ids_row[:, at] = packed[0:8, :]
    ids_col[...] = jnp.transpose(jnp.broadcast_to(ids_row[0:1, :], (LANES, 4 * rows)))
    key, value = qkv[:, HD : 2 * HD], qkv[:, 2 * HD :]
    x = place[1]
    side = x + 1 - 2 * (x % 2)
    columns = (x, 3 - x, side, 3 - side)
    for n in range(4):
        at = slice(n * rows, (n + 1) * rows)
        scores = lax.dot_general(
            qkv[at, :HD], key, (((1,), (1,)), ((), ())), preferred_element_type=F32
        )
        same = ids_col[at, 0:1] == ids_row[0:1, :]
        masked = jnp.where(same, scores, -1e30)
        top = jnp.max(masked, axis=-1, keepdims=True)
        weights = jnp.exp2((masked - top) * (HD ** (-0.5) * LOG2_E))
        scale = 1.0 / jnp.sum(weights, axis=-1, keepdims=True)
        probs = (weights * scale).astype(BF16)
        result = jnp.dot(probs, value, preferred_element_type=F32).astype(BF16)
        for z in range(per):
            out[columns[n] * per + z] = result[z * tok : (z + 1) * tok, :]


def local(packed_rows, dest_group, dest_slot, image_ids, ln_gain, qkv_weight, qk_gain):
    tok, width = packed_rows.shape
    n_dp = 2 * lax.axis_size("y")
    capacity = max(2, 2 * tok // n_dp)
    c = lax.axis_index("core")
    first_core = c == 0
    go = functools.partial(lambda array, move: send(array, n_dp, move))

    packed, qk_weight = pl.pallas_call(
        pack_body,
        out_shape=(
            jax.ShapeDtypeStruct((n_dp, capacity, width + LANES), BF16),
            jax.ShapeDtypeStruct((2, width, HD), BF16),
        ),
        in_specs=[
            pl.BlockSpec(memory_space=VMEM),
            pl.BlockSpec(memory_space=VMEM),
            pl.BlockSpec(memory_space=pltpu.HBM),
        ],
        out_specs=(pl.BlockSpec(memory_space=VMEM), pl.BlockSpec(memory_space=pltpu.HBM)),
        scratch_shapes=[pltpu.SemaphoreType.DMA],
        compiler_params=pltpu.CompilerParams(vmem_limit_bytes=32 << 20),
    )(packed_rows, jnp.stack([dest_group, dest_slot]), qkv_weight)
    near_qk = go(qk_weight, to_next)
    gain_next = go(after(qk_gain, packed), to_next)
    gain_far = go(after(qk_gain, packed), opposite_x)
    got = lax.all_to_all(packed, ("y", "core"), split_axis=0, concat_axis=0, tiled=True)
    placed = vmem_call(
        place_body, jax.ShapeDtypeStruct((tok, width + LANES), BF16), 3
    )(
        got.reshape(n_dp * capacity, width + LANES),
        image_ids.reshape(tok, 1),
        ln_gain[None, :],
    )
    placed = after(placed, near_qk, gain_next, gain_far)
    gathered = lax.all_gather(placed, ("core", "z"), axis=0, tiled=True)
    half = width // 2
    near_v = go(after(qkv_weight[2], placed), to_next)
    far = [go(after(near_qk[0], placed), on_by_side), go(after(near_qk[1], placed), on_by_mirror)]
    far.append(go(near_v[:half], on_by_side))
    far.append(go(near_v[half:], on_by_mirror))
    gain = jnp.concatenate(
        [jnp.where(first_core, qk_gain, gain_next), jnp.where(first_core, gain_next, gain_far)], axis=0
    )
    place = jnp.stack([c, lax.axis_index(("half", "side"))])

    rows = gathered.shape[0]
    step = width // 6
    steps = width // step
    whole = pl.BlockSpec((step, HD), lambda k: (k, 0))
    qkv = jax.ShapeDtypeStruct((rows // 2 + 16, 3 * HD), BF16)
    kept, *sent = pl.pallas_call(
        project_body,
        grid=(steps,),
        out_shape=(qkv,) * 5,
        in_specs=[
            pl.BlockSpec(memory_space=SMEM),
            pl.BlockSpec((rows, step), lambda k: (0, k)),
            pl.BlockSpec((rows, LANES), lambda k: (0, width // LANES)),
            pl.BlockSpec((3, step, HD), lambda k: (0, k, 0)),
            pl.BlockSpec((2, step, HD), lambda k: (0, k, 0)),
            whole,
            whole,
            whole,
            pl.BlockSpec((step, HD), lambda k: (jnp.minimum(k, steps // 2 - 1), 0)),
            pl.BlockSpec((step, HD), lambda k: (jnp.maximum(k - steps // 2, 0), 0)),
            pl.BlockSpec(memory_space=VMEM),
        ],
        out_specs=(pl.BlockSpec(memory_space=VMEM),) * 5,
        scratch_shapes=[VMEM((rows, 6 * HD), F32)],
        compiler_params=pltpu.CompilerParams(vmem_limit_bytes=48 << 20),
    )(place, gathered, gathered, qkv_weight, near_qk, near_v, *far, gain)
    swapped = [go(array, move) for array, move in zip(sent, EXCHANGE)]
    result = vmem_call(
        attend_body,
        jax.ShapeDtypeStruct((2 * rows // tok, tok, HD), BF16),
        6,
        scratch=[
            VMEM((2 * rows, 3 * HD), BF16), VMEM((8, 2 * rows), F32), VMEM((2 * rows, LANES), F32)
        ],
        smem_in=(0,),
    )(place, kept, *swapped)
    heads = lax.all_to_all(result, ("half", "side", "z"), split_axis=0, concat_axis=0, tiled=True)
    return jnp.transpose(heads, (1, 0, 2)).reshape(tok, NX * NZ * HD)


def solution(mesh):
    n_dp = mesh.devices.shape[0]
    split = Mesh(mesh.devices.reshape(n_dp // 2, 2, 2, NX // 2, NZ), AXES)
    dp, mp = ("y", "core"), ("half", "side", "z")
    return jax.shard_map(
        local,
        mesh=split,
        in_specs=(P(AXES, None), P(AXES), P(AXES), P(dp, mp), P(), P(None, None, mp), P(None, mp)),
        out_specs=P(AXES, None),
        check_vma=False,
    )
```

```python
import functools

import jax
import jax.numpy as jnp
from jax import lax
from jax.experimental import pallas as pl
from jax.experimental.pallas import tpu as pltpu
from jax.sharding import Mesh
from jax.sharding import PartitionSpec as P

HD = 128
LOG2_E = 1.4426950408889634
LANES = 128
NX, NZ = 4, 8
AXES = ("y", "core", "half", "side", "z")
BF16 = jnp.bfloat16
F32 = jnp.float32
VMEM = pltpu.VMEM
SMEM = pltpu.SMEM


def vmem_call(body, outs, n_in, scratch=(), smem_in=(), hbm_in=(), limit=48):
    spaces = [SMEM if i in smem_in else pl.ANY if i in hbm_in else VMEM for i in range(n_in)]
    return pl.pallas_call(
        body,
        out_shape=outs,
        in_specs=[pl.BlockSpec(memory_space=space) for space in spaces],
        out_specs=jax.tree.map(lambda _: pl.BlockSpec(memory_space=VMEM), outs),
        scratch_shapes=scratch,
        compiler_params=pltpu.CompilerParams(vmem_limit_bytes=limit << 20),
    )


def pairs(n_dp, move):
    out = []
    for dp in range(n_dp):
        for mp in range(NX * NZ):
            to = move(dp % 2, mp // NZ, mp % NZ)
            if to is None:
                continue
            c, x, z = to
            out.append((dp * NX * NZ + mp, (dp // 2 * 2 + c) * NX * NZ + x * NZ + z))
    return out


def send(array, n_dp, move):
    return lax.ppermute(array, AXES, pairs(n_dp, move))


def to_next(c, x, z):
    return (0, x ^ 1, z) if c == 0 else (1, 3 - x, z)


def opposite_x(c, x, z):
    return c, x ^ 2, z


def on_by_side(c, x, z):
    return (1, x ^ 1, z) if c == 1 else None


def on_by_mirror(c, x, z):
    return (1, 3 - x, z) if c == 0 else None


EXCHANGE = (
    lambda c, x, z: (1, x, z) if c == 0 else (0, 3 - x, z),
    lambda c, x, z: (0, x ^ 1, z) if c == 0 else (1, 3 - x, z),
    lambda c, x, z: (1, x ^ 1, z) if c == 0 else (0, x ^ 2, z),
    lambda c, x, z: None if c == 0 else (1, x ^ 2, z),
)


def after(array, *earlier):
    return lax.optimization_barrier((array, *earlier))[0]


def norm_rows(values, gain):
    mean = jnp.mean(values, axis=-1, keepdims=True)
    centered = values - mean
    spread = jnp.mean(centered * centered, axis=-1, keepdims=True)
    return (centered * lax.rsqrt(spread + 1e-06) * gain).astype(BF16)


def pack_body(rows, plan, gain, weight, out, q_out, k_out, v_out, parts, sem):
    depth = weight.shape[1]
    high = gain[...].astype(BF16)
    rest = gain[...] - high.astype(F32)
    middle = rest.astype(BF16)
    low = (rest - middle.astype(F32)).astype(BF16)
    pad = jnp.zeros((10, HD), F32)
    parts[...] = jnp.concatenate(
        [high.astype(F32), middle.astype(F32), low.astype(F32), pad], axis=0
    ).astype(BF16)
    copies = [
        pltpu.make_async_copy(weight.at[0], q_out, sem.at[0]),
        pltpu.make_async_copy(weight.at[1], k_out.at[pl.ds(0, depth), :], sem.at[1]),
        pltpu.make_async_copy(parts, k_out.at[pl.ds(depth, 16), :], sem.at[2]),
        pltpu.make_async_copy(weight.at[2], v_out, sem.at[3]),
    ]
    for copy in copies:
        copy.start()
    tok, width = rows.shape
    groups, capacity, _ = out.shape
    slots = groups * capacity
    group_row, slot_row = plan[0:1, :], plan[1:2, :]
    i = lax.broadcasted_iota(jnp.int32, (tok, tok), 0)
    j = lax.broadcasted_iota(jnp.int32, (tok, tok), 1)
    across = jnp.broadcast_to(group_row, (tok, tok)).astype(F32)
    down = jnp.sum(jnp.where(i == j, across, 0.0), axis=1, keepdims=True)
    rank = jnp.sum(jnp.where((down == across) & (i < j), 1, 0), axis=0, keepdims=True)
    target = group_row * capacity + rank
    hit = lax.broadcasted_iota(jnp.int32, (slots, tok), 0) == target
    onehot = jnp.where(hit, 1.0, 0.0)
    sent = jnp.dot(onehot.astype(BF16), rows[...], preferred_element_type=F32).astype(BF16)
    slot = jnp.sum(onehot * (slot_row.astype(F32) + 1.0), axis=1, keepdims=True) - 1.0
    slot = jnp.broadcast_to(slot, (slots, LANES)).astype(BF16)
    for g in range(groups):
        out[g, :, :width] = sent[g * capacity : (g + 1) * capacity, :]
        out[g, :, width:] = slot[g * capacity : (g + 1) * capacity, :]
    for copy in copies:
        copy.wait()


def place_body(got, ids_col, gain, out):
    tok = out.shape[0]
    width = out.shape[1] - LANES
    slot = got[:, width:].astype(F32)[:, :tok]
    hit = slot == lax.broadcasted_iota(jnp.int32, slot.shape, 1).astype(F32)
    onehot = jnp.where(hit, 1.0, 0.0).astype(BF16)
    grouped = lax.dot_general(
        onehot, got[:, :width], (((0,), (0,)), ((), ())), preferred_element_type=F32
    )
    out[:, :width] = norm_rows(grouped, gain[...])
    out[:, width:] = jnp.broadcast_to(ids_col[...].astype(F32), (tok, LANES)).astype(BF16)


def project_body(place, tokens, ids, own, nq, nk, nv, fq, fk, fv0, fv1, own_gain, *refs):
    parts, outs, total = refs[:2], refs[2:7], refs[7]
    k = pl.program_id(0)
    steps = pl.num_programs(0)
    rows = tokens.shape[0] // 2
    first_core = place[0] == 0
    near = [nq[...], nk[...], nv[...]]
    far = [fq[...], fk[...], jnp.where(k < steps // 2, fv0[...], fv1[...])]
    six = [jnp.where(first_core, own[j], near[j]) for j in range(3)]
    six += [jnp.where(first_core, near[j], far[j]) for j in range(3)]
    part = jnp.dot(tokens[...], jnp.concatenate(six, axis=1), preferred_element_type=F32)

    @pl.when(k == 0)
    def _():
        total[...] = part

    @pl.when(k > 0)
    def _():
        total[...] += part

    def emit(dsts):
        near_gain, far_gain = [
            p[0:2, :].astype(F32) + p[2:4, :].astype(F32) + p[4:6, :].astype(F32) for p in parts
        ]
        both = (
            jnp.where(first_core, own_gain[...], near_gain),
            jnp.where(first_core, near_gain, far_gain),
        )
        gains = [rows_of[j : j + 1, :] for rows_of in both for j in range(2)]
        turned = jnp.transpose(ids[...].astype(F32))[0:16, :].astype(BF16)
        for n, dst in enumerate(dsts):
            head, group = n // 2, n % 2
            at = slice(group * rows, (group + 1) * rows)
            for j in range(2):
                cols = total[at, (3 * head + j) * HD : (3 * head + j + 1) * HD]
                dst[:rows, j * HD : (j + 1) * HD] = norm_rows(cols, gains[2 * head + j])
            dst[:rows, 2 * HD :] = total[at, (3 * head + 2) * HD : (3 * head + 3) * HD].astype(BF16)
            dst[rows:, :rows] = turned[:, at]
            dst[rows:, rows:] = jnp.zeros((16, 3 * HD - rows), BF16)

    @pl.when((k == steps - 1) & first_core)
    def _():
        emit(outs[:4])
        outs[4][...] = jnp.zeros_like(outs[4])

    @pl.when((k == steps - 1) & jnp.logical_not(first_core))
    def _():
        outs[0][...] = jnp.zeros_like(outs[0])
        emit(outs[1:])


def attend_body(place, kept, got0, got1, got2, got3, out, qkv, ids_row, ids_col):
    rows = kept.shape[0] - 16
    tok = out.shape[1]
    per = rows // tok
    first_core = place[0] == 0
    for n, (a, b) in enumerate(((kept, got0), (got0, got1), (got1, got2), (got2, got3))):
        at = slice(n * rows, (n + 1) * rows)
        qkv[at, :] = jnp.where(first_core, a[:rows, :], b[:rows, :])
        packed = jnp.where(first_core, a[rows:, :rows], b[rows:, :rows]).astype(F32)
        ids_row[:, at] = packed[0:8, :]
    ids_col[...] = jnp.transpose(jnp.broadcast_to(ids_row[0:1, :], (LANES, 4 * rows)))
    key, value = qkv[:, HD : 2 * HD], qkv[:, 2 * HD :]
    x = place[1]
    side = x + 1 - 2 * (x % 2)
    columns = (x, 3 - x, side, 3 - side)
    for n in range(4):
        at = slice(n * rows, (n + 1) * rows)
        scores = lax.dot_general(
            qkv[at, :HD], key, (((1,), (1,)), ((), ())), preferred_element_type=F32
        )
        same = ids_col[at, 0:1] == ids_row[0:1, :]
        masked = jnp.where(same, scores, -1e30)
        top = jnp.max(masked, axis=-1, keepdims=True)
        weights = jnp.exp2((masked - top) * (HD ** (-0.5) * LOG2_E))
        scale = 1.0 / jnp.sum(weights, axis=-1, keepdims=True)
        probs = (weights * scale).astype(BF16)
        result = jnp.dot(probs, value, preferred_element_type=F32).astype(BF16)
        for z in range(per):
            out[columns[n] * per + z] = result[z * tok : (z + 1) * tok, :]


def local(packed_rows, dest_group, dest_slot, image_ids, ln_gain, qkv_weight, qk_gain):
    tok, width = packed_rows.shape
    n_dp = 2 * lax.axis_size("y")
    capacity = max(2, 2 * tok // n_dp)
    c = lax.axis_index("core")
    first_core = c == 0
    go = functools.partial(lambda array, move: send(array, n_dp, move))

    packed, q_weight, k_weight, v_weight = pl.pallas_call(
        pack_body,
        out_shape=(
            jax.ShapeDtypeStruct((n_dp, capacity, width + LANES), BF16),
            jax.ShapeDtypeStruct((width, HD), BF16),
            jax.ShapeDtypeStruct((width + 16, HD), BF16),
            jax.ShapeDtypeStruct((width, HD), BF16),
        ),
        in_specs=[pl.BlockSpec(memory_space=VMEM)] * 3 + [pl.BlockSpec(memory_space=pltpu.HBM)],
        out_specs=(
            pl.BlockSpec(memory_space=VMEM),
            pl.BlockSpec(memory_space=pltpu.HBM),
            pl.BlockSpec(memory_space=pltpu.HBM),
            pl.BlockSpec(memory_space=pltpu.HBM),
        ),
        scratch_shapes=[VMEM((16, HD), BF16), pltpu.SemaphoreType.DMA((4,))],
        compiler_params=pltpu.CompilerParams(vmem_limit_bytes=32 << 20),
    )(packed_rows, jnp.stack([dest_group, dest_slot]), qk_gain, qkv_weight)
    near_q = go(q_weight, to_next)
    near_k = go(k_weight, to_next)
    got = lax.all_to_all(packed, ("y", "core"), split_axis=0, concat_axis=0, tiled=True)
    placed = vmem_call(
        place_body, jax.ShapeDtypeStruct((tok, width + LANES), BF16), 3
    )(
        got.reshape(n_dp * capacity, width + LANES),
        image_ids.reshape(tok, 1),
        ln_gain[None, :],
    )
    placed = after(after(placed, near_q), near_k)
    gathered = lax.all_gather(placed, ("core", "z"), axis=0, tiled=True)
    half = width // 2
    near_v = go(after(v_weight, placed), to_next)
    far = [go(after(near_q, placed), on_by_side), go(after(near_k, placed), on_by_mirror)]
    far.append(go(near_v[:half], on_by_side))
    far.append(go(near_v[half:], on_by_mirror))
    place = jnp.stack([c, lax.axis_index(("half", "side"))])

    rows = gathered.shape[0]
    step = width // 6
    steps = width // step
    qkv = jax.ShapeDtypeStruct((rows // 2 + 16, 3 * HD), BF16)

    def on(core, k, place, low=0, high=steps):
        return jnp.where(place[0] == core, jnp.clip(k - low, 0, high - low - 1), 0)

    def block_of(core, low=0, high=steps):
        return pl.BlockSpec((step, HD), lambda k, place: (on(core, k, place, low, high), 0))

    near_block = pl.BlockSpec((step, HD), lambda k, place: (k, 0))
    tail = pl.BlockSpec((16, HD), lambda k, place: (width // 16, 0))
    kept, *sent = pl.pallas_call(
        project_body,
        out_shape=(qkv,) * 5,
        grid_spec=pltpu.PrefetchScalarGridSpec(
            num_scalar_prefetch=1,
            grid=(steps,),
            in_specs=[
                pl.BlockSpec((rows, step), lambda k, place: (0, k)),
                pl.BlockSpec((rows, LANES), lambda k, place: (0, width // LANES)),
                pl.BlockSpec((3, step, HD), lambda k, place: (0, on(0, k, place), 0)),
                near_block,
                near_block,
                near_block,
                block_of(1),
                block_of(1),
                block_of(1, 0, steps // 2),
                block_of(1, steps // 2),
                pl.BlockSpec(memory_space=VMEM),
                tail,
                tail,
            ],
            out_specs=(pl.BlockSpec(memory_space=VMEM),) * 5,
            scratch_shapes=[VMEM((rows, 6 * HD), F32)],
        ),
        compiler_params=pltpu.CompilerParams(vmem_limit_bytes=48 << 20),
    )(
        place, gathered, gathered, qkv_weight, near_q, near_k, near_v, *far, qk_gain, near_k, far[1]
    )
    swapped = [go(array, move) for array, move in zip(sent, EXCHANGE)]
    result = vmem_call(
        attend_body,
        jax.ShapeDtypeStruct((2 * rows // tok, tok, HD), BF16),
        6,
        scratch=[
            VMEM((2 * rows, 3 * HD), BF16), VMEM((8, 2 * rows), F32), VMEM((2 * rows, LANES), F32)
        ],
        smem_in=(0,),
    )(place, kept, *swapped)
    heads = lax.all_to_all(result, ("half", "side", "z"), split_axis=0, concat_axis=0, tiled=True)
    return jnp.transpose(heads, (1, 0, 2)).reshape(tok, NX * NZ * HD)


def solution(mesh):
    n_dp = mesh.devices.shape[0]
    split = Mesh(mesh.devices.reshape(n_dp // 2, 2, 2, NX // 2, NZ), AXES)
    dp, mp = ("y", "core"), ("half", "side", "z")
    return jax.shard_map(
        local,
        mesh=split,
        in_specs=(P(AXES, None), P(AXES), P(AXES), P(dp, mp), P(), P(None, None, mp), P(None, mp)),
        out_specs=P(AXES, None),
        check_vma=False,
    )
```

```python
import functools

import jax
import jax.numpy as jnp
from jax import lax
from jax.experimental import pallas as pl
from jax.experimental.pallas import tpu as pltpu
from jax.sharding import Mesh
from jax.sharding import PartitionSpec as P

HD = 128
LOG2_E = 1.4426950408889634
LANES = 128
NX, NZ = 4, 8
AXES = ("y", "core", "half", "side", "z")
BF16 = jnp.bfloat16
F32 = jnp.float32
VMEM = pltpu.VMEM
SMEM = pltpu.SMEM


def vmem_call(body, outs, n_in, scratch=(), smem_in=(), hbm_in=(), limit=48):
    spaces = [SMEM if i in smem_in else pl.ANY if i in hbm_in else VMEM for i in range(n_in)]
    return pl.pallas_call(
        body,
        out_shape=outs,
        in_specs=[pl.BlockSpec(memory_space=space) for space in spaces],
        out_specs=jax.tree.map(lambda _: pl.BlockSpec(memory_space=VMEM), outs),
        scratch_shapes=scratch,
        compiler_params=pltpu.CompilerParams(vmem_limit_bytes=limit << 20),
    )


def pairs(n_dp, move):
    out = []
    for dp in range(n_dp):
        for mp in range(NX * NZ):
            to = move(dp % 2, mp // NZ, mp % NZ)
            if to is None:
                continue
            c, x, z = to
            out.append((dp * NX * NZ + mp, (dp // 2 * 2 + c) * NX * NZ + x * NZ + z))
    return out


def send(array, n_dp, move):
    return lax.ppermute(array, AXES, pairs(n_dp, move))


def to_next(c, x, z):
    return (0, x ^ 1, z) if c == 0 else (1, 3 - x, z)


def opposite_x(c, x, z):
    return c, x ^ 2, z


def on_by_side(c, x, z):
    return (1, x ^ 1, z) if c == 1 else None


def on_by_mirror(c, x, z):
    return (1, 3 - x, z) if c == 0 else None


EXCHANGE = (
    lambda c, x, z: (1, x, z) if c == 0 else (0, 3 - x, z),
    lambda c, x, z: (0, x ^ 1, z) if c == 0 else (1, 3 - x, z),
    lambda c, x, z: (1, x ^ 1, z) if c == 0 else (0, x ^ 2, z),
    lambda c, x, z: None if c == 0 else (1, x ^ 2, z),
)


def after(array, *earlier):
    return lax.optimization_barrier((array, *earlier))[0]


def norm_rows(values, gain):
    mean = jnp.mean(values, axis=-1, keepdims=True)
    centered = values - mean
    spread = jnp.mean(centered * centered, axis=-1, keepdims=True)
    return (centered * lax.rsqrt(spread + 1e-06) * gain).astype(BF16)


def pack_body(rows, plan, weight, out, first_two, last, sem):
    copies = [
        pltpu.make_async_copy(weight.at[0:2], first_two, sem.at[0]),
        pltpu.make_async_copy(weight.at[2], last, sem.at[1]),
    ]
    for copy in copies:
        copy.start()
    tok, width = rows.shape
    groups, capacity, _ = out.shape
    slots = groups * capacity
    group_row, slot_row = plan[0:1, :], plan[1:2, :]
    i = lax.broadcasted_iota(jnp.int32, (tok, tok), 0)
    j = lax.broadcasted_iota(jnp.int32, (tok, tok), 1)
    across = jnp.broadcast_to(group_row, (tok, tok)).astype(F32)
    down = jnp.sum(jnp.where(i == j, across, 0.0), axis=1, keepdims=True)
    rank = jnp.sum(jnp.where((down == across) & (i < j), 1, 0), axis=0, keepdims=True)
    target = group_row * capacity + rank
    hit = lax.broadcasted_iota(jnp.int32, (slots, tok), 0) == target
    onehot = jnp.where(hit, 1.0, 0.0)
    sent = jnp.dot(onehot.astype(BF16), rows[...], preferred_element_type=F32).astype(BF16)
    slot = jnp.sum(onehot * (slot_row.astype(F32) + 1.0), axis=1, keepdims=True) - 1.0
    slot = jnp.broadcast_to(slot, (slots, LANES)).astype(BF16)
    for g in range(groups):
        out[g, :, :width] = sent[g * capacity : (g + 1) * capacity, :]
        out[g, :, width:] = slot[g * capacity : (g + 1) * capacity, :]
    for copy in copies:
        copy.wait()


def place_body(got, ids_col, gain, out):
    tok = out.shape[0]
    width = out.shape[1] - LANES
    slot = got[:, width:].astype(F32)[:, :tok]
    hit = slot == lax.broadcasted_iota(jnp.int32, slot.shape, 1).astype(F32)
    onehot = jnp.where(hit, 1.0, 0.0).astype(BF16)
    grouped = lax.dot_general(
        onehot, got[:, :width], (((0,), (0,)), ((), ())), preferred_element_type=F32
    )
    out[:, :width] = norm_rows(grouped, gain[...])
    out[:, width:] = jnp.broadcast_to(ids_col[...].astype(F32), (tok, LANES)).astype(BF16)


def project_body(place, tokens, ids, own, nqk, nv, fq, fk, fv0, fv1, gain, *refs):
    outs, total = refs[:5], refs[5]
    k = pl.program_id(0)
    steps = pl.num_programs(0)
    rows = tokens.shape[0] // 2
    first_core = place[0] == 0
    near = [nqk[0], nqk[1], nv[...]]
    far = [fq[...], fk[...], jnp.where(k < steps // 2, fv0[...], fv1[...])]
    six = [jnp.where(first_core, own[j], near[j]) for j in range(3)]
    six += [jnp.where(first_core, near[j], far[j]) for j in range(3)]
    part = jnp.dot(tokens[...], jnp.concatenate(six, axis=1), preferred_element_type=F32)

    @pl.when(k == 0)
    def _():
        total[...] = part

    @pl.when(k > 0)
    def _():
        total[...] += part

    def emit(dsts):
        turned = jnp.transpose(ids[...].astype(F32))[0:16, :].astype(BF16)
        for n, dst in enumerate(dsts):
            head, group = n // 2, n % 2
            at = slice(group * rows, (group + 1) * rows)
            for j in range(2):
                cols = total[at, (3 * head + j) * HD : (3 * head + j + 1) * HD]
                dst[:rows, j * HD : (j + 1) * HD] = norm_rows(
                    cols, gain[2 * head + j : 2 * head + j + 1, :]
                )
            dst[:rows, 2 * HD :] = total[at, (3 * head + 2) * HD : (3 * head + 3) * HD].astype(BF16)
            dst[rows:, :rows] = turned[:, at]
            dst[rows:, rows:] = jnp.zeros((16, 3 * HD - rows), BF16)

    @pl.when((k == steps - 1) & first_core)
    def _():
        emit(outs[:4])
        outs[4][...] = jnp.zeros_like(outs[4])

    @pl.when((k == steps - 1) & jnp.logical_not(first_core))
    def _():
        outs[0][...] = jnp.zeros_like(outs[0])
        emit(outs[1:])


def attend_body(place, kept, got0, got1, got2, got3, out, qkv, ids_row, ids_col):
    rows = kept.shape[0] - 16
    tok = out.shape[1]
    per = rows // tok
    first_core = place[0] == 0
    for n, (a, b) in enumerate(((kept, got0), (got0, got1), (got1, got2), (got2, got3))):
        at = slice(n * rows, (n + 1) * rows)
        qkv[at, :] = jnp.where(first_core, a[:rows, :], b[:rows, :])
        packed = jnp.where(first_core, a[rows:, :rows], b[rows:, :rows]).astype(F32)
        ids_row[:, at] = packed[0:8, :]
    ids_col[...] = jnp.transpose(jnp.broadcast_to(ids_row[0:1, :], (LANES, 4 * rows)))
    key, value = qkv[:, HD : 2 * HD], qkv[:, 2 * HD :]
    x = place[1]
    side = x + 1 - 2 * (x % 2)
    columns = (x, 3 - x, side, 3 - side)
    for n in range(4):
        at = slice(n * rows, (n + 1) * rows)
        scores = lax.dot_general(
            qkv[at, :HD], key, (((1,), (1,)), ((), ())), preferred_element_type=F32
        )
        same = ids_col[at, 0:1] == ids_row[0:1, :]
        masked = jnp.where(same, scores, -1e30)
        top = jnp.max(masked, axis=-1, keepdims=True)
        weights = jnp.exp2((masked - top) * (HD ** (-0.5) * LOG2_E))
        scale = 1.0 / jnp.sum(weights, axis=-1, keepdims=True)
        probs = (weights * scale).astype(BF16)
        result = jnp.dot(probs, value, preferred_element_type=F32).astype(BF16)
        for z in range(per):
            out[columns[n] * per + z] = result[z * tok : (z + 1) * tok, :]


def local(packed_rows, dest_group, dest_slot, image_ids, ln_gain, qkv_weight, qk_gain):
    tok, width = packed_rows.shape
    n_dp = 2 * lax.axis_size("y")
    capacity = max(2, 2 * tok // n_dp)
    c = lax.axis_index("core")
    first_core = c == 0
    go = functools.partial(lambda array, move: send(array, n_dp, move))

    packed, qk_weight, v_weight = pl.pallas_call(
        pack_body,
        out_shape=(
            jax.ShapeDtypeStruct((n_dp, capacity, width + LANES), BF16),
            jax.ShapeDtypeStruct((2, width, HD), BF16),
            jax.ShapeDtypeStruct((width, HD), BF16),
        ),
        in_specs=[
            pl.BlockSpec(memory_space=VMEM),
            pl.BlockSpec(memory_space=VMEM),
            pl.BlockSpec(memory_space=pltpu.HBM),
        ],
        out_specs=(
            pl.BlockSpec(memory_space=VMEM),
            pl.BlockSpec(memory_space=pltpu.HBM),
            pl.BlockSpec(memory_space=pltpu.HBM),
        ),
        scratch_shapes=[pltpu.SemaphoreType.DMA((2,))],
        compiler_params=pltpu.CompilerParams(vmem_limit_bytes=32 << 20),
    )(packed_rows, jnp.stack([dest_group, dest_slot]), qkv_weight)
    near_qk = go(qk_weight, to_next)
    gain_next = go(after(qk_gain, packed), to_next)
    gain_far = go(after(qk_gain, packed), opposite_x)
    got = lax.all_to_all(packed, ("y", "core"), split_axis=0, concat_axis=0, tiled=True)
    placed = vmem_call(
        place_body, jax.ShapeDtypeStruct((tok, width + LANES), BF16), 3
    )(
        got.reshape(n_dp * capacity, width + LANES),
        image_ids.reshape(tok, 1),
        ln_gain[None, :],
    )
    placed = after(placed, near_qk, gain_next, gain_far)
    gathered = lax.all_gather(placed, ("core", "z"), axis=0, tiled=True)
    half = width // 2
    near_v = go(v_weight, to_next)
    far = [go(after(near_qk[0], placed), on_by_side), go(after(near_qk[1], placed), on_by_mirror)]
    far.append(go(near_v[:half], on_by_side))
    far.append(go(near_v[half:], on_by_mirror))
    gain = jnp.concatenate(
        [jnp.where(first_core, qk_gain, gain_next), jnp.where(first_core, gain_next, gain_far)], axis=0
    )
    place = jnp.stack([c, lax.axis_index(("half", "side"))])

    rows = gathered.shape[0]
    step = width // 4
    steps = width // step
    whole = pl.BlockSpec((step, HD), lambda k: (k, 0))
    qkv = jax.ShapeDtypeStruct((rows // 2 + 16, 3 * HD), BF16)
    kept, *sent = pl.pallas_call(
        project_body,
        grid=(steps,),
        out_shape=(qkv,) * 5,
        in_specs=[
            pl.BlockSpec(memory_space=SMEM),
            pl.BlockSpec((rows, step), lambda k: (0, k)),
            pl.BlockSpec((rows, LANES), lambda k: (0, width // LANES)),
            pl.BlockSpec((3, step, HD), lambda k: (0, k, 0)),
            pl.BlockSpec((2, step, HD), lambda k: (0, k, 0)),
            whole,
            whole,
            whole,
            pl.BlockSpec((step, HD), lambda k: (jnp.minimum(k, steps // 2 - 1), 0)),
            pl.BlockSpec((step, HD), lambda k: (jnp.maximum(k - steps // 2, 0), 0)),
            pl.BlockSpec(memory_space=VMEM),
        ],
        out_specs=(pl.BlockSpec(memory_space=VMEM),) * 5,
        scratch_shapes=[VMEM((rows, 6 * HD), F32)],
        compiler_params=pltpu.CompilerParams(vmem_limit_bytes=48 << 20),
    )(place, gathered, gathered, qkv_weight, near_qk, near_v, *far, gain)
    swapped = [go(array, move) for array, move in zip(sent, EXCHANGE)]
    result = vmem_call(
        attend_body,
        jax.ShapeDtypeStruct((2 * rows // tok, tok, HD), BF16),
        6,
        scratch=[
            VMEM((2 * rows, 3 * HD), BF16), VMEM((8, 2 * rows), F32), VMEM((2 * rows, LANES), F32)
        ],
        smem_in=(0,),
    )(place, kept, *swapped)
    heads = lax.all_to_all(result, ("half", "side", "z"), split_axis=0, concat_axis=0, tiled=True)
    return jnp.transpose(heads, (1, 0, 2)).reshape(tok, NX * NZ * HD)


def solution(mesh):
    n_dp = mesh.devices.shape[0]
    split = Mesh(mesh.devices.reshape(n_dp // 2, 2, 2, NX // 2, NZ), AXES)
    dp, mp = ("y", "core"), ("half", "side", "z")
    return jax.shard_map(
        local,
        mesh=split,
        in_specs=(P(AXES, None), P(AXES), P(AXES), P(dp, mp), P(), P(None, None, mp), P(None, mp)),
        out_specs=P(AXES, None),
        check_vma=False,
    )
```

```python
import functools

import jax
import jax.numpy as jnp
from jax import lax
from jax.experimental import pallas as pl
from jax.experimental.pallas import tpu as pltpu
from jax.sharding import Mesh
from jax.sharding import PartitionSpec as P

HD = 128
LOG2_E = 1.4426950408889634
LANES = 128
NX, NZ = 4, 8
AXES = ("y", "core", "half", "side", "z")
BF16 = jnp.bfloat16
F32 = jnp.float32
VMEM = pltpu.VMEM
SMEM = pltpu.SMEM


def vmem_call(body, outs, n_in, scratch=(), smem_in=(), hbm_in=(), limit=48):
    spaces = [SMEM if i in smem_in else pl.ANY if i in hbm_in else VMEM for i in range(n_in)]
    return pl.pallas_call(
        body,
        out_shape=outs,
        in_specs=[pl.BlockSpec(memory_space=space) for space in spaces],
        out_specs=jax.tree.map(lambda _: pl.BlockSpec(memory_space=VMEM), outs),
        scratch_shapes=scratch,
        compiler_params=pltpu.CompilerParams(vmem_limit_bytes=limit << 20),
    )


def pairs(n_dp, move):
    out = []
    for dp in range(n_dp):
        for mp in range(NX * NZ):
            to = move(dp % 2, mp // NZ, mp % NZ)
            if to is None:
                continue
            c, x, z = to
            out.append((dp * NX * NZ + mp, (dp // 2 * 2 + c) * NX * NZ + x * NZ + z))
    return out


def send(array, n_dp, move):
    return lax.ppermute(array, AXES, pairs(n_dp, move))


def to_next(c, x, z):
    return (0, x ^ 1, z) if c == 0 else (1, 3 - x, z)


def on_by_side(c, x, z):
    return (1, x ^ 1, z) if c == 1 else None


def on_by_mirror(c, x, z):
    return (1, 3 - x, z) if c == 0 else None


EXCHANGE = (
    lambda c, x, z: (1, x, z) if c == 0 else (0, 3 - x, z),
    lambda c, x, z: (0, x ^ 1, z) if c == 0 else (1, 3 - x, z),
    lambda c, x, z: (1, x ^ 1, z) if c == 0 else (0, x ^ 2, z),
    lambda c, x, z: None if c == 0 else (1, x ^ 2, z),
)


def after(array, *earlier):
    return lax.optimization_barrier((array, *earlier))[0]


def norm_rows(values, gain):
    mean = jnp.mean(values, axis=-1, keepdims=True)
    centered = values - mean
    spread = jnp.mean(centered * centered, axis=-1, keepdims=True)
    return (centered * lax.rsqrt(spread + 1e-06) * gain).astype(BF16)


def pack_body(rows, plan, gain, weight, out, first_two, last, parts, sem):
    depth = weight.shape[1]
    high = gain[...].astype(BF16)
    rest = gain[...] - high.astype(F32)
    middle = rest.astype(BF16)
    low = (rest - middle.astype(F32)).astype(BF16)
    pad = jnp.zeros((10, HD), F32)
    parts[...] = jnp.concatenate(
        [high.astype(F32), middle.astype(F32), low.astype(F32), pad], axis=0
    ).astype(BF16)
    copies = [
        pltpu.make_async_copy(weight.at[0:2], first_two, sem.at[0]),
        pltpu.make_async_copy(weight.at[2], last.at[pl.ds(0, depth), :], sem.at[1]),
        pltpu.make_async_copy(parts, last.at[pl.ds(depth, 16), :], sem.at[2]),
    ]
    for copy in copies:
        copy.start()
    tok, width = rows.shape
    groups, capacity, _ = out.shape
    slots = groups * capacity
    group_row, slot_row = plan[0:1, :], plan[1:2, :]
    i = lax.broadcasted_iota(jnp.int32, (tok, tok), 0)
    j = lax.broadcasted_iota(jnp.int32, (tok, tok), 1)
    across = jnp.broadcast_to(group_row, (tok, tok)).astype(F32)
    down = jnp.sum(jnp.where(i == j, across, 0.0), axis=1, keepdims=True)
    rank = jnp.sum(jnp.where((down == across) & (i < j), 1, 0), axis=0, keepdims=True)
    target = group_row * capacity + rank
    hit = lax.broadcasted_iota(jnp.int32, (slots, tok), 0) == target
    onehot = jnp.where(hit, 1.0, 0.0)
    sent = jnp.dot(onehot.astype(BF16), rows[...], preferred_element_type=F32).astype(BF16)
    slot = jnp.sum(onehot * (slot_row.astype(F32) + 1.0), axis=1, keepdims=True) - 1.0
    slot = jnp.broadcast_to(slot, (slots, LANES)).astype(BF16)
    for g in range(groups):
        out[g, :, :width] = sent[g * capacity : (g + 1) * capacity, :]
        out[g, :, width:] = slot[g * capacity : (g + 1) * capacity, :]
    for copy in copies:
        copy.wait()


def place_body(got, ids_col, gain, out):
    tok = out.shape[0]
    width = out.shape[1] - LANES
    slot = got[:, width:].astype(F32)[:, :tok]
    hit = slot == lax.broadcasted_iota(jnp.int32, slot.shape, 1).astype(F32)
    onehot = jnp.where(hit, 1.0, 0.0).astype(BF16)
    grouped = lax.dot_general(
        onehot, got[:, :width], (((0,), (0,)), ((), ())), preferred_element_type=F32
    )
    out[:, :width] = norm_rows(grouped, gain[...])
    out[:, width:] = jnp.broadcast_to(ids_col[...].astype(F32), (tok, LANES)).astype(BF16)


def project_body(place, tokens, ids, own, nqk, nv, fq, fk, fv0, fv1, own_gain, *refs):
    parts, outs, total = refs[:2], refs[2:7], refs[7]
    k = pl.program_id(0)
    steps = pl.num_programs(0)
    rows = tokens.shape[0] // 2
    first_core = place[0] == 0
    near = [nqk[0], nqk[1], nv[...]]
    far = [fq[...], fk[...], jnp.where(k < steps // 2, fv0[...], fv1[...])]
    six = [jnp.where(first_core, own[j], near[j]) for j in range(3)]
    six += [jnp.where(first_core, near[j], far[j]) for j in range(3)]
    part = jnp.dot(tokens[...], jnp.concatenate(six, axis=1), preferred_element_type=F32)

    @pl.when(k == 0)
    def _():
        total[...] = part

    @pl.when(k > 0)
    def _():
        total[...] += part

    def emit(dsts):
        near_gain, far_gain = [
            p[0:2, :].astype(F32) + p[2:4, :].astype(F32) + p[4:6, :].astype(F32) for p in parts
        ]
        gains = (
            jnp.where(first_core, own_gain[...], near_gain),
            jnp.where(first_core, near_gain, far_gain),
        )
        turned = jnp.transpose(ids[...].astype(F32))[0:16, :].astype(BF16)
        for n, dst in enumerate(dsts):
            head, group = n // 2, n % 2
            at = slice(group * rows, (group + 1) * rows)
            for j in range(2):
                cols = total[at, (3 * head + j) * HD : (3 * head + j + 1) * HD]
                dst[:rows, j * HD : (j + 1) * HD] = norm_rows(
                    cols, gains[head][j : j + 1, :]
                )
            dst[:rows, 2 * HD :] = total[at, (3 * head + 2) * HD : (3 * head + 3) * HD].astype(BF16)
            dst[rows:, :rows] = turned[:, at]
            dst[rows:, rows:] = jnp.zeros((16, 3 * HD - rows), BF16)

    @pl.when((k == steps - 1) & first_core)
    def _():
        emit(outs[:4])
        outs[4][...] = jnp.zeros_like(outs[4])

    @pl.when((k == steps - 1) & jnp.logical_not(first_core))
    def _():
        outs[0][...] = jnp.zeros_like(outs[0])
        emit(outs[1:])


def attend_body(place, kept, got0, got1, got2, got3, out, qkv, ids_row, ids_col):
    rows = kept.shape[0] - 16
    tok = out.shape[1]
    per = rows // tok
    first_core = place[0] == 0
    for n, (a, b) in enumerate(((kept, got0), (got0, got1), (got1, got2), (got2, got3))):
        at = slice(n * rows, (n + 1) * rows)
        qkv[at, :] = jnp.where(first_core, a[:rows, :], b[:rows, :])
        packed = jnp.where(first_core, a[rows:, :rows], b[rows:, :rows]).astype(F32)
        ids_row[:, at] = packed[0:8, :]
    ids_col[...] = jnp.transpose(jnp.broadcast_to(ids_row[0:1, :], (LANES, 4 * rows)))
    key, value = qkv[:, HD : 2 * HD], qkv[:, 2 * HD :]
    x = place[1]
    side = x + 1 - 2 * (x % 2)
    columns = (x, 3 - x, side, 3 - side)
    for n in range(4):
        at = slice(n * rows, (n + 1) * rows)
        scores = lax.dot_general(
            qkv[at, :HD], key, (((1,), (1,)), ((), ())), preferred_element_type=F32
        )
        same = ids_col[at, 0:1] == ids_row[0:1, :]
        masked = jnp.where(same, scores, -1e30)
        top = jnp.max(masked, axis=-1, keepdims=True)
        weights = jnp.exp2((masked - top) * (HD ** (-0.5) * LOG2_E))
        scale = 1.0 / jnp.sum(weights, axis=-1, keepdims=True)
        probs = (weights * scale).astype(BF16)
        result = jnp.dot(probs, value, preferred_element_type=F32).astype(BF16)
        for z in range(per):
            out[columns[n] * per + z] = result[z * tok : (z + 1) * tok, :]


def local(packed_rows, dest_group, dest_slot, image_ids, ln_gain, qkv_weight, qk_gain):
    tok, width = packed_rows.shape
    n_dp = 2 * lax.axis_size("y")
    capacity = max(2, 2 * tok // n_dp)
    c = lax.axis_index("core")
    first_core = c == 0
    go = functools.partial(lambda array, move: send(array, n_dp, move))

    packed, qk_weight, v_weight = pl.pallas_call(
        pack_body,
        out_shape=(
            jax.ShapeDtypeStruct((n_dp, capacity, width + LANES), BF16),
            jax.ShapeDtypeStruct((2, width, HD), BF16),
            jax.ShapeDtypeStruct((width + 16, HD), BF16),
        ),
        in_specs=[
            pl.BlockSpec(memory_space=VMEM),
            pl.BlockSpec(memory_space=VMEM),
            pl.BlockSpec(memory_space=VMEM),
            pl.BlockSpec(memory_space=pltpu.HBM),
        ],
        out_specs=(
            pl.BlockSpec(memory_space=VMEM),
            pl.BlockSpec(memory_space=pltpu.HBM),
            pl.BlockSpec(memory_space=pltpu.HBM),
        ),
        scratch_shapes=[VMEM((16, HD), BF16), pltpu.SemaphoreType.DMA((3,))],
        compiler_params=pltpu.CompilerParams(vmem_limit_bytes=32 << 20),
    )(packed_rows, jnp.stack([dest_group, dest_slot]), qk_gain, qkv_weight)
    near_qk = go(qk_weight, to_next)
    got = lax.all_to_all(packed, ("y", "core"), split_axis=0, concat_axis=0, tiled=True)
    placed = vmem_call(
        place_body, jax.ShapeDtypeStruct((tok, width + LANES), BF16), 3
    )(
        got.reshape(n_dp * capacity, width + LANES),
        image_ids.reshape(tok, 1),
        ln_gain[None, :],
    )
    placed = after(placed, near_qk)
    gathered = lax.all_gather(placed, ("core", "z"), axis=0, tiled=True)
    half = width // 2
    near_v = go(v_weight, to_next)
    far = [go(after(near_qk[0], placed), on_by_side), go(after(near_qk[1], placed), on_by_mirror)]
    far.append(go(near_v[:half], on_by_side))
    far.append(go(near_v[half:], on_by_mirror))
    place = jnp.stack([c, lax.axis_index(("half", "side"))])

    rows = gathered.shape[0]
    step = width // 4
    steps = width // step
    whole = pl.BlockSpec((step, HD), lambda k: (k, 0))
    qkv = jax.ShapeDtypeStruct((rows // 2 + 16, 3 * HD), BF16)
    kept, *sent = pl.pallas_call(
        project_body,
        grid=(steps,),
        out_shape=(qkv,) * 5,
        in_specs=[
            pl.BlockSpec(memory_space=SMEM),
            pl.BlockSpec((rows, step), lambda k: (0, k)),
            pl.BlockSpec((rows, LANES), lambda k: (0, width // LANES)),
            pl.BlockSpec((3, step, HD), lambda k: (0, k, 0)),
            pl.BlockSpec((2, step, HD), lambda k: (0, k, 0)),
            whole,
            whole,
            whole,
            pl.BlockSpec((step, HD), lambda k: (jnp.minimum(k, steps // 2 - 1), 0)),
            pl.BlockSpec((step, HD), lambda k: (jnp.maximum(k - steps // 2, 0), 0)),
            pl.BlockSpec(memory_space=VMEM),
            pl.BlockSpec((16, HD), lambda k: (width // 16, 0)),
            pl.BlockSpec((16, HD), lambda k: (half // 16, 0)),
        ],
        out_specs=(pl.BlockSpec(memory_space=VMEM),) * 5,
        scratch_shapes=[VMEM((rows, 6 * HD), F32)],
        compiler_params=pltpu.CompilerParams(vmem_limit_bytes=48 << 20),
    )(place, gathered, gathered, qkv_weight, near_qk, near_v, *far, qk_gain, near_v, far[3])
    swapped = [go(array, move) for array, move in zip(sent, EXCHANGE)]
    result = vmem_call(
        attend_body,
        jax.ShapeDtypeStruct((2 * rows // tok, tok, HD), BF16),
        6,
        scratch=[
            VMEM((2 * rows, 3 * HD), BF16), VMEM((8, 2 * rows), F32), VMEM((2 * rows, LANES), F32)
        ],
        smem_in=(0,),
    )(place, kept, *swapped)
    heads = lax.all_to_all(result, ("half", "side", "z"), split_axis=0, concat_axis=0, tiled=True)
    return jnp.transpose(heads, (1, 0, 2)).reshape(tok, NX * NZ * HD)


def solution(mesh):
    n_dp = mesh.devices.shape[0]
    split = Mesh(mesh.devices.reshape(n_dp // 2, 2, 2, NX // 2, NZ), AXES)
    dp, mp = ("y", "core"), ("half", "side", "z")
    return jax.shard_map(
        local,
        mesh=split,
        in_specs=(P(AXES, None), P(AXES), P(AXES), P(dp, mp), P(), P(None, None, mp), P(None, mp)),
        out_specs=P(AXES, None),
        check_vma=False,
    )
```
